32 devices in a mesh: grp: 2 (over y), row: 8 (over z, x), col: 2 (over core).
Axes of the slice: x: 2, y: 2, z: 4, core: 2. Of those that a mesh axis runs over, the one named last changes fastest.
Arguments:
- queries: bfloat16 [8192, 2, 128], P(('grp', 'row', 'col')), parts along dimension 0, may hold values from -6 to 6
- keys: bfloat16 [8192, 2, 128], P(('grp', 'row', 'col')), parts along dimension 0, may hold values from -6 to 6
- values: bfloat16 [8192, 2, 128], P(('grp', 'row', 'col')), parts along dimension 0, may hold values from -6 to 6
Outputs:
- attended: bfloat16 [8192, 256], P(('grp', 'row', 'col')), parts along dimension 0
The draws below stay inside these ranges and needn't reach their ends.
There are 2 independent parts, one for each index of `grp`. The reference program is written for one: setup_inputs(seed, part) draws one part's arguments, and reference() takes and returns one part's arrays. A program takes and returns all parts, laid end to end along the dimension named above; each array names one. Nothing has to cross between parts.
All inputs are finite; a program needn't handle non-finite values.
Results may differ from the reference program's by a relative error of at most 0.014.
Values may be sent and summed in bfloat16 or wider, within the bound.
A program may use at most 128 MiB of HBM per device.

```python
import jax
import jax.numpy as jnp
from jax import lax

HEAD = 128
HEADS = 2
TOKENS = 4096


def make_pairs(key):
    first, second = jax.random.split(jax.random.fold_in(key, 7), 2)
    shape = (TOKENS, HEADS, HEAD)
    query_draw = jnp.clip(jax.random.normal(first, shape, jnp.float32) * 1.732, -6.0, 6.0)
    key_draw = jnp.clip(jax.random.normal(second, shape, jnp.float32) * 1.732, -6.0, 6.0)
    return (query_draw, key_draw)


def draw_queries(key, part):
    return make_pairs(key)[0].astype(jnp.bfloat16)


def draw_keys(key, part):
    return make_pairs(key)[1].astype(jnp.bfloat16)


def level_of(rng, shape, shards, smallest, high):
    factor_of, own = 1.0, jax.random.fold_in(rng, 6)
    for axis_at, blocks in shards:
        steps = jnp.exp(jax.random.uniform(jax.random.fold_in(own, axis_at), (blocks,), jnp.float32, smallest / len(shards), high / len(shards)))
        factor_of = factor_of * jnp.repeat(steps, shape[axis_at] // blocks).reshape([-1 if axis == axis_at else 1 for axis in range(len(shape))])
    return factor_of


def scatter_about(own_key, dims, deviation, limit, shards=(), kind=jnp.bfloat16):
    level = level_of(own_key, dims, shards, -0.22, 0.18) if shards else 1.0
    values = jax.random.normal(own_key, dims, jnp.float32) * deviation * level
    return jnp.minimum(jnp.maximum(values, -limit), limit).astype(kind)


def setup_inputs(seed: int = 0, part: int = 0) -> dict:
    arg_keys = jax.random.split(jax.random.key(seed), 4)
    part_splits = jax.random.split(jax.random.fold_in(arg_keys[3], part), 4)
    return {
        "queries": draw_queries(jax.random.fold_in(jax.random.fold_in(arg_keys[3], part), 71), part),
        "keys": draw_keys(jax.random.fold_in(jax.random.fold_in(arg_keys[3], part), 71), part),
        "values": scatter_about(part_splits[2], (TOKENS, HEADS, HEAD), 1.0, 6.0, ((0, 16),)),
    }


def reference(queries, keys, values):
    scale = HEAD ** -0.5
    key_full = keys.astype(jnp.float32)
    value_full = values.astype(jnp.float32)
    length = min(512, TOKENS)
    query_blocks = queries.reshape(TOKENS // length, length, HEADS, HEAD)

    def one_block(query_block):
        score = jnp.einsum("qhd,khd->hqk", query_block.astype(jnp.float32), key_full, precision=lax.Precision.HIGHEST) * scale
        peak = jnp.max(score, axis=-1)
        weight = jnp.exp(score - peak[..., None]).astype(jnp.bfloat16)
        total = jnp.sum(weight.astype(jnp.float32), axis=-1)
        mixed = jnp.einsum("hqk,khd->qhd", weight.astype(jnp.float32), value_full, precision=lax.Precision.HIGHEST)
        result = mixed / jnp.transpose(total)[..., None]
        return result.reshape(length, HEADS * HEAD).astype(jnp.bfloat16)

    return lax.map(one_block, query_blocks).reshape(TOKENS, HEADS * HEAD)
```

```python
import functools
import math

import jax
import jax.numpy as jnp
from jax import lax
from jax.experimental import pallas as pl
from jax.experimental.pallas import tpu as pltpu
from jax.sharding import PartitionSpec as P

MESH = pl.DeviceIdType.MESH


def kernel(
    rows, cores, q_ref, k_ref, v_ref, o_ref,
    stage, kv, qs, part, stat, got, got_stat, peak, total, accum,
    own_send, own_recv, pair_send, fwd_send, kv_recv, q_send, q_recv,
    out_send, out_recv, stat_send, stat_recv,
):
    tokens, heads, width = q_ref.shape
    group = rows // 2
    bits = [1 << n for n in range(group.bit_length() - 1)]
    span = cores * tokens
    rate = width ** -0.5 * math.log2(math.e)

    r = lax.axis_index("row")
    c = lax.axis_index("col")
    sib = lax.rem(c + 1, cores)
    far = lax.rem(r + group, rows)

    def across(bit):
        return r + bit * (1 - 2 * lax.rem(r // bit, 2))

    def at(row, core):
        return {"row": row, "col": core}

    barrier = pltpu.get_barrier_semaphore()
    pl.semaphore_signal(barrier, inc=1, device_id=at(r, sib), device_id_type=MESH)
    for row in [across(bit) for bit in bits] + [far]:
        for h in range(cores):
            pl.semaphore_signal(barrier, inc=1, device_id=at(row, h), device_id_type=MESH)

    for h in range(heads):
        stage[h, 0] = k_ref[:, h, :]
        stage[h, 1] = v_ref[:, h, :]
        stage[h, 2] = q_ref[:, h, :]
    pl.semaphore_wait(barrier, 1 + cores * (len(bits) + 1))

    def remote(src, dst, send, recv, row, core):
        return pltpu.make_async_remote_copy(
            src_ref=src, dst_ref=dst, send_sem=send, recv_sem=recv,
            device_id=at(row, core), device_id_type=MESH,
        )

    sends = []

    def go(copy):
        copy.start()
        sends.append(copy)

    kv_sib = remote(stage.at[sib, pl.ds(0, 2)], kv.at[0, c], own_send.at[0], own_recv.at[0], r, sib)
    q_sib = remote(stage.at[sib, 2], qs.at[0, c], own_send.at[1], own_recv.at[1], r, sib)
    go(kv_sib)
    go(q_sib)
    for n in reversed(range(len(bits))):
        for h in range(cores):
            go(remote(
                stage.at[h, pl.ds(0, 2)], kv.at[bits[n], c], pair_send.at[n, h],
                kv_recv.at[bits[n], c], across(bits[n]), h,
            ))
    for h in range(cores):
        go(remote(stage.at[h, 2], qs.at[1, c], q_send.at[h], q_recv.at[c], far, h))

    kv[0, c] = stage[c, 0:2]
    qs[0, c] = stage[c, 2]

    peak[...] = jnp.full_like(peak, -1e30)
    total[...] = jnp.zeros_like(total)
    accum[...] = jnp.zeros_like(accum)

    def tile(i, j):
        q = qs[i].reshape(span, width)
        k = kv[j, :, 0].reshape(span, width)
        v = kv[j, :, 1].reshape(span, width)
        s = lax.dot_general(q, k, (((1,), (1,)), ((), ())), preferred_element_type=jnp.float32)
        before = peak[i]
        now = jnp.maximum(before, jnp.max(s, axis=-1, keepdims=True))
        fade = jnp.exp2((before - now) * rate)
        w = jnp.exp2((s - now) * rate).astype(jnp.bfloat16)
        peak[i] = now
        total[i] = total[i] * fade + jnp.sum(w.astype(jnp.float32), axis=-1, keepdims=True)
        accum[i] = accum[i] * fade + jnp.dot(w, v, preferred_element_type=jnp.float32)

    def tiles(i, low, high):
        if high - low == 1:
            tile(i, low)
        else:
            pl.loop(low, high)(lambda j: tile(i, j))

    def finish(i):
        done = accum[i] / total[i]
        level = peak[i] * rate + jnp.log2(total[i])
        flat = jnp.broadcast_to(level, (span, 128)).T[0:8]
        return done.astype(jnp.bfloat16), flat

    def arrived(j):
        for s in range(cores):
            remote(stage.at[0, pl.ds(0, 2)], kv.at[j, s], own_send.at[0], kv_recv.at[j, s], r, sib).wait_recv()
            for n, bit in enumerate(bits):
                if j % (2 * bit) == 0:
                    go(remote(
                        kv.at[j, s], kv.at[j + bit, s], fwd_send.at[j, n, s],
                        kv_recv.at[j + bit, s], across(bit), c,
                    ))

    kv_sib.wait_recv()
    q_sib.wait_recv()
    tiles(0, 0, 1)
    order = sorted(range(1, group), key=lambda j: (bin(j).count("1"), -j))
    for j in order[:-1]:
        arrived(j)
    tiles(0, 1, group - 1)
    for s in range(cores):
        remote(stage.at[0, 2], qs.at[1, s], q_send.at[0], q_recv.at[s], r, sib).wait_recv()
    tiles(1, 0, group - 1)
    arrived(order[-1])
    tiles(1, group - 1, group)

    done, flat = finish(1)
    for s in range(cores):
        part[1, s] = done[s * tokens:(s + 1) * tokens]
        stat[1, s] = flat[:, s * tokens:(s + 1) * tokens]
        go(remote(stat.at[1, s], got_stat.at[1, c], stat_send.at[1, s], stat_recv.at[1, c], far, s))
        go(remote(part.at[1, s], got.at[1, c], out_send.at[1, s], out_recv.at[1, c], far, s))

    tiles(0, group - 1, group)
    done, flat = finish(0)
    for s in range(cores):
        part[0, s] = done[s * tokens:(s + 1) * tokens]
        stat[0, s] = flat[:, s * tokens:(s + 1) * tokens]
    stat_sib = remote(stat.at[0, sib], got_stat.at[0, c], stat_send.at[0, 0], stat_recv.at[0, 0], r, sib)
    out_sib = remote(part.at[0, sib], got.at[0, c], out_send.at[0, 0], out_recv.at[0, 0], r, sib)
    go(stat_sib)
    go(out_sib)
    got[0, c] = part[0, c]
    got_stat[0, c] = stat[0, c]
    stat_sib.wait_recv()
    out_sib.wait_recv()
    for h in range(cores):
        remote(stat.at[1, 0], got_stat.at[1, h], stat_send.at[1, 0], stat_recv.at[1, h], r, sib).wait_recv()
        remote(part.at[1, 0], got.at[1, h], out_send.at[1, 0], out_recv.at[1, h], r, sib).wait_recv()
    for h in range(heads):
        one, two = got_stat[0, h], got_stat[1, h]
        top = jnp.maximum(one, two)
        one, two = jnp.exp2(one - top), jnp.exp2(two - top)
        share = one / (one + two)
        share = jnp.broadcast_to(share[0:1], (128, tokens)).T
        near, away = got[0, h].astype(jnp.float32), got[1, h].astype(jnp.float32)
        o_ref[:, h * width:(h + 1) * width] = (away + (near - away) * share).astype(o_ref.dtype)
    for copy in sends:
        copy.wait_send()


def solution(mesh):
    rows, cores = mesh.shape["row"], mesh.shape["col"]
    group = rows // 2
    levels = group.bit_length() - 1

    def body(queries, keys, values):
        tokens, heads, width = queries.shape
        span = cores * tokens
        dma = pltpu.SemaphoreType.DMA
        bf16, f32 = jnp.bfloat16, jnp.float32
        return pl.pallas_call(
            functools.partial(kernel, rows, cores),
            out_shape=jax.ShapeDtypeStruct((tokens, heads * width), bf16),
            in_specs=[pl.BlockSpec(memory_space=pltpu.VMEM)] * 3,
            out_specs=pl.BlockSpec(memory_space=pltpu.VMEM),
            scratch_shapes=[
                pltpu.VMEM((heads, 3, tokens, width), bf16),
                pltpu.VMEM((group, cores, 2, tokens, width), bf16),
                pltpu.VMEM((2, cores, tokens, width), bf16),
                pltpu.VMEM((2, cores, tokens, width), bf16),
                pltpu.VMEM((2, cores, 8, tokens), f32),
                pltpu.VMEM((2, heads, tokens, width), bf16),
                pltpu.VMEM((2, heads, 8, tokens), f32),
                pltpu.VMEM((2, span, 1), f32),
                pltpu.VMEM((2, span, 1), f32),
                pltpu.VMEM((2, span, width), f32),
                dma((2,)), dma((2,)), dma((levels, cores)), dma((group, levels, cores)),
                dma((group, cores)), dma((cores,)), dma((cores,)),
                dma((2, cores)), dma((2, cores)), dma((2, cores)), dma((2, cores)),
            ],
            compiler_params=pltpu.CompilerParams(
                collective_id=0, has_side_effects=True, vmem_limit_bytes=48 * 1024 * 1024
            ),
        )(queries, keys, values)

    spec = P(("grp", "row", "col"), None, None)
    return jax.shard_map(
        body, mesh=mesh, in_specs=(spec,) * 3,
        out_specs=P(("grp", "row", "col"), None), check_vma=False,
    )
```

```python
import functools
import math

import jax
import jax.numpy as jnp
from jax import lax
from jax.experimental import pallas as pl
from jax.experimental.pallas import tpu as pltpu
from jax.sharding import PartitionSpec as P

MESH = pl.DeviceIdType.MESH


def kernel(
    rows, cores, q_hbm, k_hbm, v_hbm, o_ref,
    raw, stage, kv, qs, part, stat, got, got_stat, peak, total, accum,
    load, own_send, own_recv, pair_send, fwd_send, kv_recv, q_send, q_recv,
    out_send, out_recv, stat_send, stat_recv,
):
    tokens, heads, width = q_hbm.shape
    group = rows // 2
    bits = [1 << n for n in range(group.bit_length() - 1)]
    span = cores * tokens
    rate = width ** -0.5 * math.log2(math.e)

    loads = [
        pltpu.make_async_copy(ref, raw.at[n], load.at[n])
        for n, ref in enumerate((k_hbm, v_hbm, q_hbm))
    ]
    for copy in loads:
        copy.start()

    r = lax.axis_index("row")
    c = lax.axis_index("col")
    sib = lax.rem(c + 1, cores)
    far = lax.rem(r + group, rows)

    def across(bit):
        return r + bit * (1 - 2 * lax.rem(r // bit, 2))

    def at(row, core):
        return {"row": row, "col": core}

    barrier = pltpu.get_barrier_semaphore()
    pl.semaphore_signal(barrier, inc=1, device_id=at(r, sib), device_id_type=MESH)
    for row in [across(bit) for bit in bits] + [far]:
        for h in range(cores):
            pl.semaphore_signal(barrier, inc=1, device_id=at(row, h), device_id_type=MESH)

    for n, copy in enumerate(loads):
        copy.wait()
        for h in range(heads):
            stage[h, n] = raw[n, :, h, :]
    pl.semaphore_wait(barrier, 1 + cores * (len(bits) + 1))

    def remote(src, dst, send, recv, row, core):
        return pltpu.make_async_remote_copy(
            src_ref=src, dst_ref=dst, send_sem=send, recv_sem=recv,
            device_id=at(row, core), device_id_type=MESH,
        )

    sends = []

    def go(copy):
        copy.start()
        sends.append(copy)

    kv_sib = remote(stage.at[sib, pl.ds(0, 2)], kv.at[0, c], own_send.at[0], own_recv.at[0], r, sib)
    q_sib = remote(stage.at[sib, 2], qs.at[0, c], own_send.at[1], own_recv.at[1], r, sib)
    go(kv_sib)
    go(q_sib)
    for n in reversed(range(len(bits))):
        for h in range(cores):
            go(remote(
                stage.at[h, pl.ds(0, 2)], kv.at[bits[n], c], pair_send.at[n, h],
                kv_recv.at[bits[n], c], across(bits[n]), h,
            ))
    for h in range(cores):
        go(remote(stage.at[h, 2], qs.at[1, c], q_send.at[h], q_recv.at[c], far, h))

    kv[0, c] = stage[c, 0:2]
    qs[0, c] = stage[c, 2]

    peak[...] = jnp.full_like(peak, -1e30)
    total[...] = jnp.zeros_like(total)
    accum[...] = jnp.zeros_like(accum)

    def tile(i, s, j):
        k = kv[j, :, 0].reshape(span, width)
        v = kv[j, :, 1].reshape(span, width)
        scores = lax.dot_general(
            qs[i, s], k, (((1,), (1,)), ((), ())), preferred_element_type=jnp.float32
        )
        before = peak[i, s]
        now = jnp.maximum(before, jnp.max(scores, axis=-1, keepdims=True))
        fade = jnp.exp2((before - now) * rate)
        w = jnp.exp2((scores - now) * rate).astype(jnp.bfloat16)
        peak[i, s] = now
        total[i, s] = total[i, s] * fade + jnp.sum(w.astype(jnp.float32), axis=-1, keepdims=True)
        accum[i, s] = accum[i, s] * fade + jnp.dot(w, v, preferred_element_type=jnp.float32)

    def tiles(i, low, high, parts=range(cores)):
        def step(j):
            for s in parts:
                tile(i, s, j)

        if high - low == 1:
            step(low)
        else:
            pl.loop(low, high)(step)

    def finish(i, s):
        part[i, s] = (accum[i, s] / total[i, s]).astype(jnp.bfloat16)
        level = peak[i, s] * rate + jnp.log2(total[i, s])
        stat[i, s] = jnp.broadcast_to(level, (tokens, 128)).T[0:8]

    def arrived(j):
        for s in range(cores):
            remote(stage.at[0, pl.ds(0, 2)], kv.at[j, s], own_send.at[0], kv_recv.at[j, s], r, sib).wait_recv()
            for n, bit in enumerate(bits):
                if j % (2 * bit) == 0:
                    go(remote(
                        kv.at[j, s], kv.at[j + bit, s], fwd_send.at[j, n, s],
                        kv_recv.at[j + bit, s], across(bit), c,
                    ))

    kv_sib.wait_recv()
    q_sib.wait_recv()
    tiles(0, 0, 1)
    order = sorted(range(1, group), key=lambda j: (bin(j).count("1"), -j))
    for j in order[:-1]:
        arrived(j)
    tiles(0, 1, group - 1)
    for s in range(cores):
        remote(stage.at[0, 2], qs.at[1, s], q_send.at[0], q_recv.at[s], r, sib).wait_recv()
    tiles(1, 0, group - 1)
    arrived(order[-1])
    for s in range(cores):
        tiles(1, group - 1, group, (s,))
        finish(1, s)
        go(remote(stat.at[1, s], got_stat.at[1, c], stat_send.at[1, s], stat_recv.at[1, c], far, s))
        go(remote(part.at[1, s], got.at[1, c], out_send.at[1, s], out_recv.at[1, c], far, s))

    tiles(0, group - 1, group)
    for s in range(cores):
        finish(0, s)
    stat_sib = remote(stat.at[0, sib], got_stat.at[0, c], stat_send.at[0, 0], stat_recv.at[0, 0], r, sib)
    out_sib = remote(part.at[0, sib], got.at[0, c], out_send.at[0, 0], out_recv.at[0, 0], r, sib)
    go(stat_sib)
    go(out_sib)
    got[0, c] = part[0, c]
    got_stat[0, c] = stat[0, c]
    stat_sib.wait_recv()
    out_sib.wait_recv()
    for h in range(cores):
        remote(stat.at[1, 0], got_stat.at[1, h], stat_send.at[1, 0], stat_recv.at[1, h], r, sib).wait_recv()
        remote(part.at[1, 0], got.at[1, h], out_send.at[1, 0], out_recv.at[1, h], r, sib).wait_recv()
    for h in range(heads):
        one, two = got_stat[0, h], got_stat[1, h]
        top = jnp.maximum(one, two)
        one, two = jnp.exp2(one - top), jnp.exp2(two - top)
        share = one / (one + two)
        share = jnp.broadcast_to(share[0:1], (128, tokens)).T
        near, away = got[0, h].astype(jnp.float32), got[1, h].astype(jnp.float32)
        o_ref[:, h * width:(h + 1) * width] = (away + (near - away) * share).astype(o_ref.dtype)
    for copy in sends:
        copy.wait_send()


def solution(mesh):
    rows, cores = mesh.shape["row"], mesh.shape["col"]
    group = rows // 2
    levels = group.bit_length() - 1

    def body(queries, keys, values):
        tokens, heads, width = queries.shape
        dma = pltpu.SemaphoreType.DMA
        bf16, f32 = jnp.bfloat16, jnp.float32
        return pl.pallas_call(
            functools.partial(kernel, rows, cores),
            out_shape=jax.ShapeDtypeStruct((tokens, heads * width), bf16),
            in_specs=[pl.BlockSpec(memory_space=pltpu.HBM)] * 3,
            out_specs=pl.BlockSpec(memory_space=pltpu.VMEM),
            scratch_shapes=[
                pltpu.VMEM((3, tokens, heads, width), bf16),
                pltpu.VMEM((heads, 3, tokens, width), bf16),
                pltpu.VMEM((group, cores, 2, tokens, width), bf16),
                pltpu.VMEM((2, cores, tokens, width), bf16),
                pltpu.VMEM((2, cores, tokens, width), bf16),
                pltpu.VMEM((2, cores, 8, tokens), f32),
                pltpu.VMEM((2, heads, tokens, width), bf16),
                pltpu.VMEM((2, heads, 8, tokens), f32),
                pltpu.VMEM((2, cores, tokens, 1), f32),
                pltpu.VMEM((2, cores, tokens, 1), f32),
                pltpu.VMEM((2, cores, tokens, width), f32),
                dma((3,)), dma((2,)), dma((2,)), dma((levels, cores)), dma((group, levels, cores)),
                dma((group, cores)), dma((cores,)), dma((cores,)),
                dma((2, cores)), dma((2, cores)), dma((2, cores)), dma((2, cores)),
            ],
            compiler_params=pltpu.CompilerParams(
                collective_id=0, has_side_effects=True, vmem_limit_bytes=63 * 1024 * 1024
            ),
        )(queries, keys, values)

    spec = P(("grp", "row", "col"), None, None)
    return jax.shard_map(
        body, mesh=mesh, in_specs=(spec,) * 3,
        out_specs=P(("grp", "row", "col"), None), check_vma=False,
    )
```

```python
import functools
import math

import jax
import jax.numpy as jnp
from jax import lax
from jax.experimental import pallas as pl
from jax.experimental.pallas import tpu as pltpu
from jax.sharding import PartitionSpec as P

MESH = pl.DeviceIdType.MESH


def kernel(
    rows, cores, q_hbm, k_hbm, v_hbm, o_ref,
    raw, stage, kv, qs, part, stat, got, got_stat, peak, total, accum,
    load, own_send, own_recv, pair_send, fwd_send, kv_recv, q_send, q_recv,
    out_send, out_recv, stat_send, stat_recv,
):
    tokens, heads, width = q_hbm.shape
    group = rows // 2
    bits = [1 << n for n in range(group.bit_length() - 1)]
    span = cores * tokens
    rate = width ** -0.5 * math.log2(math.e)

    loads = [
        pltpu.make_async_copy(ref, raw.at[n], load.at[n])
        for n, ref in enumerate((k_hbm, v_hbm, q_hbm))
    ]
    for copy in loads:
        copy.start()

    r = lax.axis_index("row")
    c = lax.axis_index("col")
    sib = lax.rem(c + 1, cores)
    far = lax.rem(r + group, rows)

    def across(bit):
        return r + bit * (1 - 2 * lax.rem(r // bit, 2))

    def at(row, core):
        return {"row": row, "col": core}

    barrier = pltpu.get_barrier_semaphore()
    pl.semaphore_signal(barrier, inc=1, device_id=at(r, sib), device_id_type=MESH)
    for row in [across(bit) for bit in bits] + [far]:
        for h in range(cores):
            pl.semaphore_signal(barrier, inc=1, device_id=at(row, h), device_id_type=MESH)

    for n, copy in enumerate(loads):
        copy.wait()
        for h in range(heads):
            stage[h, n] = raw[n, :, h, :]
    pl.semaphore_wait(barrier, 1 + cores * (len(bits) + 1))

    def remote(src, dst, send, recv, row, core):
        return pltpu.make_async_remote_copy(
            src_ref=src, dst_ref=dst, send_sem=send, recv_sem=recv,
            device_id=at(row, core), device_id_type=MESH,
        )

    sends = []

    def go(copy):
        copy.start()
        sends.append(copy)

    kv_sib = remote(stage.at[sib, pl.ds(0, 2)], kv.at[0, c], own_send.at[0], own_recv.at[0], r, sib)
    q_sib = remote(stage.at[sib, 2], qs.at[0, c], own_send.at[1], own_recv.at[1], r, sib)
    go(kv_sib)
    go(q_sib)
    for n in reversed(range(len(bits))):
        for h in range(cores):
            go(remote(
                stage.at[h, pl.ds(0, 2)], kv.at[bits[n], c], pair_send.at[n, h],
                kv_recv.at[bits[n], c], across(bits[n]), h,
            ))
    for h in range(cores):
        go(remote(stage.at[h, 2], qs.at[1, c], q_send.at[h], q_recv.at[c], far, h))

    kv[0, c] = stage[c, 0:2]
    qs[0, c] = stage[c, 2]

    peak[...] = jnp.full_like(peak, -1e30)
    total[...] = jnp.zeros_like(total)
    accum[...] = jnp.zeros_like(accum)

    def tile(i, s, j):
        k = kv[j, :, 0].reshape(span, width)
        v = kv[j, :, 1].reshape(span, width)
        scores = lax.dot_general(
            qs[i, s], k, (((1,), (1,)), ((), ())), preferred_element_type=jnp.float32
        )
        before = peak[i, s]
        now = jnp.maximum(before, jnp.max(scores, axis=-1, keepdims=True))
        fade = jnp.exp2((before - now) * rate)
        w = jnp.exp2((scores - now) * rate).astype(jnp.bfloat16)
        peak[i, s] = now
        total[i, s] = total[i, s] * fade + jnp.sum(w.astype(jnp.float32), axis=-1, keepdims=True)
        accum[i, s] = accum[i, s] * fade + jnp.dot(w, v, preferred_element_type=jnp.float32)

    def tiles(i, low, high, parts=range(cores)):
        def step(j):
            for s in parts:
                tile(i, s, j)

        if high - low == 1:
            step(low)
        else:
            pl.loop(low, high)(step)

    def finish(i, s):
        part[i, s] = (accum[i, s] / total[i, s]).astype(jnp.bfloat16)
        level = peak[i, s] * rate + jnp.log2(total[i, s])
        stat[i, s] = jnp.broadcast_to(level, (tokens, 128)).T[0:8]

    def arrived(j):
        for s in range(cores):
            remote(stage.at[0, pl.ds(0, 2)], kv.at[j, s], own_send.at[0], kv_recv.at[j, s], r, sib).wait_recv()
            for n, bit in enumerate(bits):
                if j % (2 * bit) == 0:
                    go(remote(
                        kv.at[j, s], kv.at[j + bit, s], fwd_send.at[j, n, s],
                        kv_recv.at[j + bit, s], across(bit), c,
                    ))

    kv_sib.wait_recv()
    q_sib.wait_recv()
    tiles(0, 0, 1)
    order = sorted(range(1, group), key=lambda j: (bin(j).count("1"), -j))
    for j in order[:-1]:
        arrived(j)
    tiles(0, 1, group - 1)
    for s in range(cores):
        remote(stage.at[0, 2], qs.at[1, s], q_send.at[0], q_recv.at[s], r, sib).wait_recv()
    tiles(1, 0, group - 1)
    arrived(order[-1])
    for s in range(cores):
        tiles(1, group - 1, group, (s,))
        finish(1, s)
        go(remote(stat.at[1, s], got_stat.at[1, c], stat_send.at[1, s], stat_recv.at[1, c], far, s))
        go(remote(part.at[1, s], got.at[1, c], out_send.at[1, s], out_recv.at[1, c], far, s))

    tiles(0, group - 1, group)
    for s in range(cores):
        finish(0, s)
    stat_sib = remote(stat.at[0, sib], got_stat.at[0, c], stat_send.at[0, 0], stat_recv.at[0, 0], r, sib)
    out_sib = remote(part.at[0, sib], got.at[0, c], out_send.at[0, 0], out_recv.at[0, 0], r, sib)
    go(stat_sib)
    go(out_sib)
    got[0, c] = part[0, c]
    got_stat[0, c] = stat[0, c]
    stat_sib.wait_recv()
    out_sib.wait_recv()
    for h in range(cores):
        remote(stat.at[1, 0], got_stat.at[1, h], stat_send.at[1, 0], stat_recv.at[1, h], r, sib).wait_recv()
        remote(part.at[1, 0], got.at[1, h], out_send.at[1, 0], out_recv.at[1, h], r, sib).wait_recv()
    for h in range(heads):
        one, two = got_stat[0, h], got_stat[1, h]
        top = jnp.maximum(one, two)
        one, two = jnp.exp2(one - top), jnp.exp2(two - top)
        share = one / (one + two)
        share = jnp.broadcast_to(share[0:1], (128, tokens)).T
        near, away = got[0, h].astype(jnp.float32), got[1, h].astype(jnp.float32)
        o_ref[:, h * width:(h + 1) * width] = (away + (near - away) * share).astype(o_ref.dtype)
    for copy in sends:
        copy.wait_send()


def solution(mesh):
    rows, cores = mesh.shape["row"], mesh.shape["col"]
    group = rows // 2
    levels = group.bit_length() - 1

    def body(queries, keys, values):
        tokens, heads, width = queries.shape
        dma = pltpu.SemaphoreType.DMA
        bf16, f32 = jnp.bfloat16, jnp.float32
        return pl.pallas_call(
            functools.partial(kernel, rows, cores),
            out_shape=jax.ShapeDtypeStruct((tokens, heads * width), bf16),
            in_specs=[pl.BlockSpec(memory_space=pltpu.HBM)] * 3,
            out_specs=pl.BlockSpec(memory_space=pltpu.VMEM),
            scratch_shapes=[
                pltpu.VMEM((3, tokens, heads, width), bf16),
                pltpu.VMEM((heads, 3, tokens, width), bf16),
                pltpu.VMEM((group, cores, 2, tokens, width), bf16),
                pltpu.VMEM((2, cores, tokens, width), bf16),
                pltpu.VMEM((2, cores, tokens, width), bf16),
                pltpu.VMEM((2, cores, 8, tokens), f32),
                pltpu.VMEM((2, heads, tokens, width), bf16),
                pltpu.VMEM((2, heads, 8, tokens), f32),
                pltpu.VMEM((2, cores, tokens, 1), f32),
                pltpu.VMEM((2, cores, tokens, 1), f32),
                pltpu.VMEM((2, cores, tokens, width), f32),
                dma((3,)), dma((2,)), dma((2,)), dma((levels, cores)), dma((group, levels, cores)),
                dma((group, cores)), dma((cores,)), dma((cores,)),
                dma((2, cores)), dma((2, cores)), dma((2, cores)), dma((2, cores)),
            ],
            compiler_params=pltpu.CompilerParams(
                collective_id=0, has_side_effects=True, vmem_limit_bytes=48 * 1024 * 1024
            ),
        )(*[pltpu.with_memory_space_constraint(x, pltpu.HBM) for x in (queries, keys, values)])

    spec = P(("grp", "row", "col"), None, None)
    return jax.shard_map(
        body, mesh=mesh, in_specs=(spec,) * 3,
        out_specs=P(("grp", "row", "col"), None), check_vma=False,
    )
```

```python
import functools
import math

import jax
import jax.numpy as jnp
from jax import lax
from jax.experimental import pallas as pl
from jax.experimental.pallas import tpu as pltpu
from jax.sharding import PartitionSpec as P

MESH = pl.DeviceIdType.MESH


def kernel(
    rows, cores, q_hbm, k_hbm, v_hbm, o_ref,
    raw, stage, kv, qs, part, stat, got, got_stat, peak, total, accum,
    load, own_send, own_recv, pair_send, fwd_send, kv_recv, q_send, q_recv,
    out_send, out_recv, stat_send, stat_recv,
):
    tokens, heads, width = q_hbm.shape
    group = rows // 2
    bits = [1 << n for n in range(group.bit_length() - 1)]
    span = cores * tokens
    rate = width ** -0.5 * math.log2(math.e)

    loads = [
        pltpu.make_async_copy(ref, raw.at[n], load.at[n])
        for n, ref in enumerate((k_hbm, v_hbm, q_hbm))
    ]
    for copy in loads:
        copy.start()

    r = lax.axis_index("row")
    c = lax.axis_index("col")
    sib = lax.rem(c + 1, cores)
    far = lax.rem(r + group, rows)

    def across(bit):
        return r + bit * (1 - 2 * lax.rem(r // bit, 2))

    def at(row, core):
        return {"row": row, "col": core}

    barrier = pltpu.get_barrier_semaphore()
    pl.semaphore_signal(barrier, inc=1, device_id=at(r, sib), device_id_type=MESH)
    for row in [across(bit) for bit in bits] + [far]:
        for h in range(cores):
            pl.semaphore_signal(barrier, inc=1, device_id=at(row, h), device_id_type=MESH)

    for n, copy in enumerate(loads):
        copy.wait()
        for h in range(heads):
            stage[h, n] = raw[n, :, h, :]
    pl.semaphore_wait(barrier, 1 + cores * (len(bits) + 1))

    def remote(src, dst, send, recv, row, core):
        return pltpu.make_async_remote_copy(
            src_ref=src, dst_ref=dst, send_sem=send, recv_sem=recv,
            device_id=at(row, core), device_id_type=MESH,
        )

    sends = []

    def go(copy):
        copy.start()
        sends.append(copy)

    kv_sib = remote(stage.at[sib, pl.ds(0, 2)], kv.at[0, c], own_send.at[0], own_recv.at[0], r, sib)
    q_sib = remote(stage.at[sib, 2], qs.at[0, c], own_send.at[1], own_recv.at[1], r, sib)
    go(kv_sib)
    go(q_sib)
    for n in reversed(range(len(bits))):
        for h in range(cores):
            go(remote(
                stage.at[h, pl.ds(0, 2)], kv.at[bits[n], c], pair_send.at[n, h],
                kv_recv.at[bits[n], c], across(bits[n]), h,
            ))
    for h in range(cores):
        go(remote(stage.at[h, 2], qs.at[1, c], q_send.at[h], q_recv.at[c], far, h))

    kv[0, c] = stage[c, 0:2]
    qs[0, c] = stage[c, 2]

    peak[...] = jnp.full_like(peak, -1e30)
    total[...] = jnp.zeros_like(total)
    accum[...] = jnp.zeros_like(accum)

    def tile(i, s, j):
        k = kv[j, :, 0].reshape(span, width)
        v = kv[j, :, 1].reshape(span, width)
        scores = lax.dot_general(
            qs[i, s], k, (((1,), (1,)), ((), ())), preferred_element_type=jnp.float32
        )
        before = peak[i, s]
        now = jnp.maximum(before, jnp.max(scores, axis=-1, keepdims=True))
        fade = jnp.exp2((before - now) * rate)
        w = jnp.exp2((scores - now) * rate).astype(jnp.bfloat16)
        peak[i, s] = now
        total[i, s] = total[i, s] * fade + jnp.sum(w.astype(jnp.float32), axis=-1, keepdims=True)
        accum[i, s] = accum[i, s] * fade + jnp.dot(w, v, preferred_element_type=jnp.float32)

    def tiles(i, low, high, parts=range(cores)):
        def step(j):
            for s in parts:
                tile(i, s, j)

        if high - low <= 4:
            for j in range(low, high):
                step(j)
        else:
            pl.loop(low, high)(step)

    def finish(i, s):
        part[i, s] = (accum[i, s] / total[i, s]).astype(jnp.bfloat16)
        level = peak[i, s] * rate + jnp.log2(total[i, s])
        stat[i, s] = jnp.broadcast_to(level, (tokens, 128)).T[0:8]

    def arrived(j):
        for s in range(cores):
            remote(stage.at[0, pl.ds(0, 2)], kv.at[j, s], own_send.at[0], kv_recv.at[j, s], r, sib).wait_recv()
            for n, bit in enumerate(bits):
                if j % (2 * bit) == 0:
                    go(remote(
                        kv.at[j, s], kv.at[j + bit, s], fwd_send.at[j, n, s],
                        kv_recv.at[j + bit, s], across(bit), c,
                    ))

    kv_sib.wait_recv()
    q_sib.wait_recv()
    tiles(0, 0, 1)
    order = sorted(range(1, group), key=lambda j: (bin(j).count("1"), -j))
    for j in order[:-1]:
        arrived(j)
    tiles(0, 1, group - 1)
    for s in range(cores):
        remote(stage.at[0, 2], qs.at[1, s], q_send.at[0], q_recv.at[s], r, sib).wait_recv()
    tiles(1, 0, group - 1)
    arrived(order[-1])
    for s in range(cores):
        tiles(1, group - 1, group, (s,))
        finish(1, s)
        go(remote(stat.at[1, s], got_stat.at[1, c], stat_send.at[1, s], stat_recv.at[1, c], far, s))
        go(remote(part.at[1, s], got.at[1, c], out_send.at[1, s], out_recv.at[1, c], far, s))

    tiles(0, group - 1, group)
    for s in range(cores):
        finish(0, s)
    stat_sib = remote(stat.at[0, sib], got_stat.at[0, c], stat_send.at[0, 0], stat_recv.at[0, 0], r, sib)
    out_sib = remote(part.at[0, sib], got.at[0, c], out_send.at[0, 0], out_recv.at[0, 0], r, sib)
    go(stat_sib)
    go(out_sib)
    got[0, c] = part[0, c]
    got_stat[0, c] = stat[0, c]
    stat_sib.wait_recv()
    out_sib.wait_recv()
    for h in range(cores):
        remote(stat.at[1, 0], got_stat.at[1, h], stat_send.at[1, 0], stat_recv.at[1, h], r, sib).wait_recv()
        remote(part.at[1, 0], got.at[1, h], out_send.at[1, 0], out_recv.at[1, h], r, sib).wait_recv()
    for h in range(heads):
        one, two = got_stat[0, h], got_stat[1, h]
        top = jnp.maximum(one, two)
        one, two = jnp.exp2(one - top), jnp.exp2(two - top)
        share = one / (one + two)
        share = jnp.broadcast_to(share[0:1], (128, tokens)).T
        near, away = got[0, h].astype(jnp.float32), got[1, h].astype(jnp.float32)
        o_ref[:, h * width:(h + 1) * width] = (away + (near - away) * share).astype(o_ref.dtype)
    for copy in sends:
        copy.wait_send()


def solution(mesh):
    rows, cores = mesh.shape["row"], mesh.shape["col"]
    group = rows // 2
    levels = group.bit_length() - 1

    def body(queries, keys, values):
        tokens, heads, width = queries.shape
        dma = pltpu.SemaphoreType.DMA
        bf16, f32 = jnp.bfloat16, jnp.float32
        return pl.pallas_call(
            functools.partial(kernel, rows, cores),
            out_shape=jax.ShapeDtypeStruct((tokens, heads * width), bf16),
            in_specs=[pl.BlockSpec(memory_space=pltpu.HBM)] * 3,
            out_specs=pl.BlockSpec(memory_space=pltpu.VMEM),
            scratch_shapes=[
                pltpu.VMEM((3, tokens, heads, width), bf16),
                pltpu.VMEM((heads, 3, tokens, width), bf16),
                pltpu.VMEM((group, cores, 2, tokens, width), bf16),
                pltpu.VMEM((2, cores, tokens, width), bf16),
                pltpu.VMEM((2, cores, tokens, width), bf16),
                pltpu.VMEM((2, cores, 8, tokens), f32),
                pltpu.VMEM((2, heads, tokens, width), bf16),
                pltpu.VMEM((2, heads, 8, tokens), f32),
                pltpu.VMEM((2, cores, tokens, 1), f32),
                pltpu.VMEM((2, cores, tokens, 1), f32),
                pltpu.VMEM((2, cores, tokens, width), f32),
                dma((3,)), dma((2,)), dma((2,)), dma((levels, cores)), dma((group, levels, cores)),
                dma((group, cores)), dma((cores,)), dma((cores,)),
                dma((2, cores)), dma((2, cores)), dma((2, cores)), dma((2, cores)),
            ],
            compiler_params=pltpu.CompilerParams(
                collective_id=0, has_side_effects=True, vmem_limit_bytes=48 * 1024 * 1024
            ),
        )(*[pltpu.with_memory_space_constraint(x, pltpu.HBM) for x in (queries, keys, values)])

    spec = P(("grp", "row", "col"), None, None)
    return jax.shard_map(
        body, mesh=mesh, in_specs=(spec,) * 3,
        out_specs=P(("grp", "row", "col"), None), check_vma=False,
    )
```
